32 devices in a mesh: groups: 2 (over x), dp: 16 (over z, y, core).
Axes of the slice: x: 2, y: 2, z: 4, core: 2. Of those that a mesh axis runs over, the one named last changes fastest.
Arguments:
- acts: bfloat16 [16384, 5120], P(('groups', 'dp')), parts along dimension 0, may hold values from -72 to 72, as said below
- out_grads: bfloat16 [16384, 2560], P(('groups', 'dp')), parts along dimension 0, may hold values from -24 to 24
- a_old: float32 [10240], P(('groups', 'dp')), parts along dimension 0, may hold values from 0.5 to 2
- eigen_old: float32 [5120], P('groups'), parts along dimension 0, may hold values from 0.005 to 2
- gradient: float32 [10240, 2560], P(('groups', 'dp')), parts along dimension 0, may hold values from -1.75 to 1.75
- basis: bfloat16 [5120, 2560], P(('groups', 'dp')), parts along dimension 0, may hold values from -0.125 to 0.125
Outputs:
- a_new: float32 [10240], P(('groups', 'dp')), parts along dimension 0
- eigen_new: float32 [5120], P('groups'), parts along dimension 0
- update: float32 [10240, 2560], P(('groups', 'dp')), parts along dimension 0
The draws below stay inside these ranges and needn't reach their ends.
There are 2 independent parts, one for each index of `groups`. The reference program is written for one: setup_inputs(seed, part) draws one part's arguments, and reference() takes and returns one part's arrays. A program takes and returns all parts, laid end to end along the dimension named above; each array names one. Nothing has to cross between parts.
Inputs may be any that keep to these rules, and one draw needn't show every extreme that they name: `acts`: each entry is a random feature value times a scale of its token and a scale of its feature.
All inputs are finite; a program needn't handle non-finite values.
Results may differ from the reference program's by a relative error of at most 0.0003.
Values may be sent and summed in bfloat16 or wider, within the bound.
A program may use at most 128 MiB of HBM per device.

```python
import math
import jax
import jax.numpy as jnp
from jax import lax

D = 5120
E = 2560
TOKENS = 8192


def draw_acts(key, part):
    key = jax.random.fold_in(key, 11)
    first, second, third = jax.random.split(key, 3)
    column_scale = jnp.exp(jax.random.uniform(second, (D,), jnp.float32, math.log(0.3), math.log(3.0)))
    position = jnp.arange(TOKENS).astype(jnp.float32) / max(TOKENS - 1, 1)
    values = jnp.clip(jax.random.normal(first, (TOKENS, D), jnp.float32), -4.0, 4.0)
    row_scale = jnp.exp(jax.random.uniform(third, (TOKENS,), jnp.float32, math.log(0.3), math.log(3.3)))
    row_scale = row_scale * jnp.sqrt(1.0 + 2.0 * position)
    return (values * row_scale[:, None] * column_scale[None, :]).astype(jnp.bfloat16)


def draw_out_grads(key, part):
    key = jax.random.fold_in(key, 37)
    first, second = jax.random.split(key, 2)
    position = jnp.arange(TOKENS).astype(jnp.float32) / max(TOKENS - 1, 1)
    values = jnp.clip(jax.random.normal(first, (TOKENS, E), jnp.float32), -4.0, 4.0)
    row_scale = jnp.exp(jax.random.uniform(second, (TOKENS,), jnp.float32, math.log(0.5), math.log(2.0)))
    row_scale = row_scale * jnp.sqrt(1.0 + 2.0 * position)
    return (values * row_scale[:, None]).astype(jnp.bfloat16)


def shard_levels(own_key, extent, cuts, smallest, high):
    gain, own = 1.0, jax.random.fold_in(own_key, 6)
    for dim, blocks in cuts:
        draws = jnp.exp(jax.random.uniform(jax.random.fold_in(own, dim), (blocks,), jnp.float32, smallest / len(cuts), high / len(cuts)))
        gain = gain * jnp.repeat(draws, extent[dim] // blocks).reshape([-1 if axis == dim else 1 for axis in range(len(extent))])
    return gain


def normal_values(key, extent, spread, limit, shards=(), kind=jnp.bfloat16):
    loudness = shard_levels(key, extent, shards, -0.22, 0.18) if shards else 1.0
    entries = jax.random.normal(key, extent, jnp.float32) * spread * loudness
    return jnp.minimum(jnp.maximum(entries, -limit), limit).astype(kind)


def setup_inputs(seed: int = 0, part: int = 0) -> dict:
    keys = jax.random.split(jax.random.key(seed), 7)
    own_keys = jax.random.split(jax.random.fold_in(keys[6], part), 7)
    return {
        "acts": draw_acts(jax.random.fold_in(jax.random.fold_in(keys[6], part), 71), part),
        "out_grads": draw_out_grads(jax.random.fold_in(jax.random.fold_in(keys[6], part), 71), part),
        "a_old": jnp.clip(jnp.exp(math.log(2.0) - 1.3862944 * jax.random.uniform(own_keys[2], (D,), jnp.float32) ** shard_levels(own_keys[2], (D,), ((0, 16),), -0.2, 0.2)), 0.5, 2.0),
        "eigen_old": jnp.clip(jnp.exp(jax.random.uniform(own_keys[3], (E,), jnp.float32, math.log(0.005), math.log(2.0))), 0.005, 2.0),
        "gradient": normal_values(own_keys[4], (D, E), 0.3, 1.75, ((0, 16),), jnp.float32),
        "basis": normal_values(own_keys[5], (E, E), E ** -0.5, 0.125, ((0, 16),)),
    }


RETAIN = 0.9
DAMPING = 0.001


def reference(acts, out_grads, a_old, eigen_old, gradient, basis):
    block = math.gcd(TOKENS, 2048)
    count = TOKENS // block
    act_blocks = acts.reshape(count, block, D)
    grad_blocks = out_grads.reshape(count, block, E)

    def add_block(carry, pieces):
        act_piece, grad_piece = pieces
        act_float = act_piece.astype(jnp.float32)
        rotated = jnp.dot(grad_piece, basis, preferred_element_type=jnp.float32)
        new_carry = (carry[0] + jnp.sum(act_float * act_float, axis=0), carry[1] + jnp.sum(rotated * rotated, axis=0))
        return new_carry, None

    start = (jnp.zeros((D,), jnp.float32), jnp.zeros((E,), jnp.float32))
    (act_total, eigen_total), _ = lax.scan(add_block, start, (act_blocks, grad_blocks))
    a_new = RETAIN * a_old + (1.0 - RETAIN) * (act_total / TOKENS)
    eigen_new = RETAIN * eigen_old + (1.0 - RETAIN) * (eigen_total / TOKENS)
    basis_float = basis.astype(jnp.float32)
    coeffs = jnp.dot(gradient, basis_float, precision=lax.Precision.HIGHEST)
    scaled = coeffs / (a_new[:, None] * eigen_new[None, :] + DAMPING)
    update = jnp.dot(scaled, basis_float.T, precision=lax.Precision.HIGHEST)
    return (a_new, eigen_new, update)
```

```python
import functools

import jax
import jax.numpy as jnp
from jax import lax
from jax.experimental import pallas as pl
from jax.experimental.pallas import tpu as pltpu
from jax.sharding import PartitionSpec as P

RETAIN = 0.9
DAMPING = 0.001
MESH = pl.DeviceIdType.MESH
CHUNKS = 5
AHEAD = 2


def split(x):
    high = x.astype(jnp.bfloat16)
    low = (x - high.astype(jnp.float32)).astype(jnp.bfloat16)
    return high, low


def kernel(
    n, tokens, acts_hbm, grads_hbm, rows_hbm, a_old, eigen_old, basis,
    a_new, eigen_new, update,
    whole, acts, lhs, rows, coeffs, damped, column, act_sums, eigen_sums,
    load_sem, send_sem, recv_sem, act_send, act_recv, eigen_send, eigen_recv,
):
    me = lax.axis_index("dp")
    group = lax.axis_index("groups")
    core = me % 2
    side = (me // 2) % 2
    layer = me // 4
    layers = n // 4
    height, features = basis.shape
    width = features // CHUNKS
    local_tokens = grads_hbm.shape[0]
    local_rows = rows_hbm.shape[0]

    def index(at_layer, at_side, at_core):
        return (at_layer * 2 + at_side) * 2 + at_core

    sibling = index(layer, side, 1 - core)
    across = index(layer, 1 - side, core)

    load_acts = pltpu.make_async_copy(acts_hbm, acts, load_sem.at[0])
    load_grads = pltpu.make_async_copy(grads_hbm, lhs.at[pl.ds(0, local_tokens), :], load_sem.at[1])
    load_rows = pltpu.make_async_copy(rows_hbm, rows, load_sem.at[2])

    barrier = pltpu.get_barrier_semaphore()

    def greet(d, _):
        pl.semaphore_signal(barrier, inc=1, device_id=(group, (me + d) % n), device_id_type=MESH)
        return _

    lax.fori_loop(1, n, greet, 0)
    load_acts.start()
    load_grads.start()
    load_rows.start()
    pl.semaphore_wait(barrier, n - 1)

    def slot(c, owner):
        return whole.at[c, pl.ds(pl.multiple_of(owner * height, 16), height), :]

    def move(c, owner, target, which, own=False):
        source = basis.at[:, pl.ds(pl.multiple_of(c * width, 128), width)] if own else slot(c, owner)
        return pltpu.make_async_remote_copy(
            src_ref=source,
            dst_ref=slot(c, owner),
            send_sem=send_sem.at[c, which],
            recv_sem=recv_sem.at[c, owner],
            device_id=(group, target),
            device_id_type=MESH,
        )

    def own_moves(c):
        moves = [move(c, me, index((layer + d) % layers, side, core), d - 1, True) for d in range(1, layers)]
        moves.append(move(c, me, across, layers - 1, True))
        moves.append(move(c, me, sibling, layers, True))
        return moves

    def layer_moves(c):
        out = []
        for d in range(1, layers):
            owner = index((layer + layers - d) % layers, side, core)
            base = layers + 1 + 2 * (d - 1)
            out.append((move(c, owner, across, base), move(c, owner, sibling, base + 1)))
        return out

    def across_moves(c):
        base = layers + 1 + 2 * (layers - 1)
        return [
            move(c, index((layer + layers - d) % layers, 1 - side, core), sibling, base + d)
            for d in range(layers)
        ]

    def send_own(c):
        for copy in own_moves(c):
            copy.start()
        whole[c, pl.ds(pl.multiple_of(me * height, 16), height), :] = basis[
            :, pl.ds(pl.multiple_of(c * width, 128), width)
        ]

    for c in range(AHEAD):
        send_own(c)

    load_acts.wait()
    act_width = 512

    def add_acts(b, _):
        columns = pl.ds(pl.multiple_of(b * act_width, 128), act_width)
        block = acts[:, columns].astype(jnp.float32)
        act_sums[me, :, columns] = jnp.sum(block * block, axis=0, keepdims=True)
        return _

    lax.fori_loop(0, acts.shape[1] // act_width, add_acts, 0)

    def act_copy(d, owner):
        return pltpu.make_async_remote_copy(
            src_ref=act_sums.at[owner],
            dst_ref=act_sums.at[owner],
            send_sem=act_send.at[d],
            recv_sem=act_recv.at[owner],
            device_id=(group, (me + d) % n),
            device_id_type=MESH,
        )

    def eigen_copy(c, d, owner):
        return pltpu.make_async_remote_copy(
            src_ref=eigen_sums.at[c, owner],
            dst_ref=eigen_sums.at[c, owner],
            send_sem=eigen_send.at[c, d],
            recv_sem=eigen_recv.at[c, owner],
            device_id=(group, (me + d) % n),
            device_id_type=MESH,
        )

    def send_acts(d, _):
        act_copy(d, me).start()
        return _

    lax.fori_loop(1, n, send_acts, 0)

    load_rows.wait()
    high, low = split(rows[...])
    lhs[pl.ds(local_tokens, local_rows), :] = high
    lhs[pl.ds(local_tokens + local_rows, local_rows), :] = low
    load_grads.wait()
    update[...] = jnp.zeros_like(update)

    def rotate(c):
        tile = 256

        def part(t, _):
            columns = pl.ds(pl.multiple_of(t * tile, 128), tile)
            out = jnp.dot(lhs[...], whole[c, :, columns], preferred_element_type=jnp.float32)
            turned = out[:local_tokens]
            eigen_sums[c, me, :, columns] = jnp.sum(turned * turned, axis=0, keepdims=True)
            coeffs[c, :, columns] = out[local_tokens : local_tokens + local_rows] + out[local_tokens + local_rows :]
            return _

        lax.fori_loop(0, width // tile, part, 0)

        def send(d, _):
            eigen_copy(c, d, me).start()
            return _

        lax.fori_loop(1, n, send, 0)

    def finish_acts():
        def arrive(d, _):
            act_copy(d, (me + n - d) % n).wait_recv()
            return _

        lax.fori_loop(1, n, arrive, 0)
        total = act_sums[0]
        for owner in range(1, n):
            total = total + act_sums[owner]
        wide = total.shape[1]
        block = 512
        picked = jnp.zeros((local_rows, 1), jnp.float32)
        for b in range(wide // block):
            at = lax.broadcasted_iota(jnp.int32, (local_rows, block), 1) + b * block
            row = lax.broadcasted_iota(jnp.int32, (local_rows, block), 0) + me * local_rows
            mine = jnp.where(at == row, jnp.broadcast_to(total[:, b * block : (b + 1) * block], at.shape), 0.0)
            picked = picked + jnp.sum(mine, axis=1, keepdims=True)
        square = (local_rows, local_rows)
        same = lax.broadcasted_iota(jnp.int32, square, 0) == lax.broadcasted_iota(jnp.int32, square, 1)
        old = jnp.sum(jnp.where(same, jnp.broadcast_to(a_old[...], square), 0.0), axis=1, keepdims=True)
        new = RETAIN * old + (1.0 - RETAIN) * (picked / tokens)
        column[...] = jnp.broadcast_to(new, column.shape)
        a_new[...] = jnp.sum(jnp.where(same, jnp.broadcast_to(new, square), 0.0), axis=0, keepdims=True)

    def back(c):
        def arrive(d, _):
            eigen_copy(c, d, (me + n - d) % n).wait_recv()
            return _

        lax.fori_loop(1, n, arrive, 0)
        total = eigen_sums[c, 0]
        for owner in range(1, n):
            total = total + eigen_sums[c, owner]
        columns = pl.ds(pl.multiple_of(c * width, 128), width)
        values = RETAIN * eigen_old[:, columns] + (1.0 - RETAIN) * (total / tokens)
        eigen_new[:, columns] = values
        scaled = coeffs[c] / (column[:, 0:1] * values + DAMPING)
        top, bottom = split(scaled)
        damped[pl.ds(0, local_rows), :] = top
        damped[pl.ds(local_rows, local_rows), :] = bottom
        tile = 256

        def part(t, _):
            here = pl.ds(pl.multiple_of(t * tile, 128), tile)
            out = lax.dot_general(
                damped[...], whole[c, here, :], (((1,), (1,)), ((), ())), preferred_element_type=jnp.float32
            )
            update[:, here] += out[:local_rows] + out[local_rows:]
            return _

        lax.fori_loop(0, features // tile, part, 0)

    def step(i, carry):
        @pl.when(i < CHUNKS)
        def _():
            for over, beside in layer_moves(i):
                over.wait_recv()
                over.start()
                beside.start()

        @pl.when(i + AHEAD < CHUNKS)
        def _():
            send_own(i + AHEAD)

        @pl.when(jnp.logical_and(i >= 1, i <= CHUNKS))
        def _():
            c = i - 1
            for copy in across_moves(c):
                copy.wait_recv()
                copy.start()
            for at_side in range(2):
                for d in range(layers):
                    owner = index(d, at_side, 1 - core)
                    move(c, owner, sibling, 0).wait_recv()
            rotate(c)

        @pl.when(i == 1)
        def _():
            finish_acts()

        @pl.when(i >= 2)
        def _():
            back(i - 2)

        return carry

    lax.fori_loop(0, CHUNKS + 2, step, 0)

    def drain(c, _):
        for copy in own_moves(c):
            copy.wait_send()
        for over, beside in layer_moves(c):
            over.wait_send()
            beside.wait_send()
        for copy in across_moves(c):
            copy.wait_send()

        def sent(d, _):
            eigen_copy(c, d, me).wait_send()
            return _

        return lax.fori_loop(1, n, sent, _)

    lax.fori_loop(0, CHUNKS, drain, 0)

    def act_sent(d, _):
        act_copy(d, me).wait_send()
        return _

    lax.fori_loop(1, n, act_sent, 0)


def fused(acts, out_grads, a_old, eigen_old, gradient, basis):
    n = lax.axis_size("dp")
    tokens = acts.shape[0] * n
    height, features = basis.shape
    width = features // CHUNKS
    local_rows = gradient.shape[0]
    depth = out_grads.shape[0] + 2 * local_rows
    wide = acts.shape[1]
    hbm = pl.BlockSpec(memory_space=pl.ANY)
    vmem = pl.BlockSpec(memory_space=pltpu.VMEM)
    copies = 4 * (n // 4)
    a_new, eigen_new, update = pl.pallas_call(
        functools.partial(kernel, n, tokens),
        out_shape=(
            jax.ShapeDtypeStruct((1, local_rows), jnp.float32),
            jax.ShapeDtypeStruct((1, features), jnp.float32),
            jax.ShapeDtypeStruct((local_rows, features), jnp.float32),
        ),
        in_specs=[hbm, hbm, hbm, vmem, vmem, vmem],
        out_specs=(vmem, vmem, vmem),
        scratch_shapes=[
            pltpu.VMEM((CHUNKS, features, width), jnp.bfloat16),
            pltpu.VMEM(acts.shape, jnp.bfloat16),
            pltpu.VMEM((depth, features), jnp.bfloat16),
            pltpu.VMEM(gradient.shape, jnp.float32),
            pltpu.VMEM((CHUNKS, local_rows, width), jnp.float32),
            pltpu.VMEM((2 * local_rows, width), jnp.bfloat16),
            pltpu.VMEM((local_rows, 128), jnp.float32),
            pltpu.VMEM((n, 1, wide), jnp.float32),
            pltpu.VMEM((CHUNKS, n, 1, width), jnp.float32),
            pltpu.SemaphoreType.DMA((3,)),
            pltpu.SemaphoreType.DMA((CHUNKS, copies)),
            pltpu.SemaphoreType.DMA((CHUNKS, n)),
            pltpu.SemaphoreType.DMA((n,)),
            pltpu.SemaphoreType.DMA((n,)),
            pltpu.SemaphoreType.DMA((CHUNKS, n)),
            pltpu.SemaphoreType.DMA((CHUNKS, n)),
        ],
        compiler_params=pltpu.CompilerParams(
            collective_id=0, has_side_effects=True, vmem_limit_bytes=56 * 1024 * 1024
        ),
    )(acts, out_grads, gradient, a_old.reshape(1, -1), eigen_old.reshape(1, -1), basis)
    return a_new.reshape(-1), eigen_new.reshape(-1), update


def plain(acts, out_grads, a_old, eigen_old, gradient, basis):
    tokens = acts.shape[0] * lax.axis_size("dp")
    own_rows = a_old.shape[0]
    act_float = acts.astype(jnp.float32)
    act_part = jnp.sum(act_float * act_float, axis=0)
    shard_rows = lax.all_gather(basis, "dp", axis=0, tiled=True)
    token_part = jnp.dot(out_grads, shard_rows, preferred_element_type=jnp.float32)
    row_part = jnp.dot(gradient, shard_rows.astype(jnp.float32), precision=lax.Precision.HIGHEST)
    eigen_part = jnp.sum(token_part * token_part, axis=0)
    act_whole, eigen_total = lax.psum((act_part, eigen_part), "dp")
    act_total = lax.dynamic_slice_in_dim(act_whole, lax.axis_index("dp") * own_rows, own_rows, 0)
    a_new = RETAIN * a_old + (1.0 - RETAIN) * (act_total / tokens)
    eigen_new = RETAIN * eigen_old + (1.0 - RETAIN) * (eigen_total / tokens)
    scaled = row_part / (a_new[:, None] * eigen_new[None, :] + DAMPING)
    update = jnp.einsum("ik,jk->ij", scaled, shard_rows.astype(jnp.float32), precision=lax.Precision.HIGHEST)
    return (a_new, eigen_new, update)


def solution(mesh):
    return jax.shard_map(
        fused if mesh.shape["dp"] == 16 else plain,
        mesh=mesh,
        in_specs=(
            P(("groups", "dp"), None),
            P(("groups", "dp"), None),
            P(("groups", "dp")),
            P("groups"),
            P(("groups", "dp"), None),
            P(("groups", "dp"), None),
        ),
        out_specs=(P(("groups", "dp")), P("groups"), P(("groups", "dp"), None)),
        check_vma=False,
    )
```

```python
import functools

import jax
import jax.numpy as jnp
from jax import lax
from jax.experimental import pallas as pl
from jax.experimental.pallas import tpu as pltpu
from jax.sharding import PartitionSpec as P

RETAIN = 0.9
DAMPING = 0.001
MESH = pl.DeviceIdType.MESH
CHUNKS = 5
AHEAD = 2


def split(x):
    high = x.astype(jnp.bfloat16)
    low = (x - high.astype(jnp.float32)).astype(jnp.bfloat16)
    return high, low


def kernel(
    n, tokens, acts_hbm, grads_hbm, rows_hbm, a_old, eigen_old, basis,
    a_new, eigen_new, update,
    whole, acts, lhs, rows, coeffs, damped, column, act_sums, eigen_sums,
    load_sem, send_sem, recv_sem, act_send, act_recv, eigen_send, eigen_recv,
):
    me = lax.axis_index("dp")
    group = lax.axis_index("groups")
    core = me % 2
    side = (me // 2) % 2
    layer = me // 4
    layers = n // 4
    height, features = basis.shape
    width = features // CHUNKS
    local_tokens = grads_hbm.shape[0]
    local_rows = rows_hbm.shape[0]

    def index(at_layer, at_side, at_core):
        return (at_layer * 2 + at_side) * 2 + at_core

    sibling = index(layer, side, 1 - core)
    across = index(layer, 1 - side, core)

    load_acts = pltpu.make_async_copy(acts_hbm, acts, load_sem.at[0])
    load_grads = pltpu.make_async_copy(grads_hbm, lhs.at[pl.ds(0, local_tokens), :], load_sem.at[1])
    load_rows = pltpu.make_async_copy(rows_hbm, rows, load_sem.at[2])

    barrier = pltpu.get_barrier_semaphore()

    def greet(d, _):
        pl.semaphore_signal(barrier, inc=1, device_id=(group, (me + d) % n), device_id_type=MESH)
        return _

    lax.fori_loop(1, n, greet, 0)
    load_acts.start()
    load_grads.start()
    load_rows.start()
    pl.semaphore_wait(barrier, n - 1)

    def slot(c, owner):
        return whole.at[c, pl.ds(pl.multiple_of(owner * height, 16), height), :]

    def move(c, owner, target, which, own=False):
        source = basis.at[:, pl.ds(pl.multiple_of(c * width, 128), width)] if own else slot(c, owner)
        return pltpu.make_async_remote_copy(
            src_ref=source,
            dst_ref=slot(c, owner),
            send_sem=send_sem.at[c, which],
            recv_sem=recv_sem.at[c, owner],
            device_id=(group, target),
            device_id_type=MESH,
        )

    def own_moves(c):
        return [
            (layer < layers - 1, move(c, me, me + 4, 0, True)),
            (layer > 0, move(c, me, me - 4, 1, True)),
            (None, move(c, me, across, 2, True)),
            (None, move(c, me, sibling, 3, True)),
        ]

    def layer_moves(c):
        out = []
        for d in range(1, layers):
            for below in (True, False):
                base = 4 + 3 * (2 * (d - 1) + (0 if below else 1))
                owner = me - 4 * d if below else me + 4 * d
                onward = me + 4 if below else me - 4
                present = layer >= d if below else layer + d < layers
                further = layer < layers - 1 if below else layer > 0
                out.append((
                    present,
                    jnp.logical_and(present, further),
                    move(c, owner, onward, base),
                    move(c, owner, across, base + 1),
                    move(c, owner, sibling, base + 2),
                ))
        return out

    def across_moves(c):
        base = 4 + 6 * (layers - 1)
        return [
            move(c, index((layer + layers - d) % layers, 1 - side, core), sibling, base + d)
            for d in range(layers)
        ]

    def run(condition, action):
        if condition is None:
            action()
        else:
            pl.when(condition)(action)

    def send_own(c):
        for condition, copy in own_moves(c):
            run(condition, copy.start)
        whole[c, pl.ds(pl.multiple_of(me * height, 16), height), :] = basis[
            :, pl.ds(pl.multiple_of(c * width, 128), width)
        ]

    def pass_on(over, beside):
        over.wait_recv()
        over.start()
        beside.start()

    for c in range(AHEAD):
        send_own(c)

    load_acts.wait()
    act_width = 512

    def add_acts(b, _):
        columns = pl.ds(pl.multiple_of(b * act_width, 128), act_width)
        block = acts[:, columns].astype(jnp.float32)
        act_sums[me, :, columns] = jnp.sum(block * block, axis=0, keepdims=True)
        return _

    lax.fori_loop(0, acts.shape[1] // act_width, add_acts, 0)

    def act_copy(d, owner):
        return pltpu.make_async_remote_copy(
            src_ref=act_sums.at[owner],
            dst_ref=act_sums.at[owner],
            send_sem=act_send.at[d],
            recv_sem=act_recv.at[owner],
            device_id=(group, (me + d) % n),
            device_id_type=MESH,
        )

    def eigen_copy(c, d, owner):
        return pltpu.make_async_remote_copy(
            src_ref=eigen_sums.at[c, owner],
            dst_ref=eigen_sums.at[c, owner],
            send_sem=eigen_send.at[c, d],
            recv_sem=eigen_recv.at[c, owner],
            device_id=(group, (me + d) % n),
            device_id_type=MESH,
        )

    def send_acts(d, _):
        act_copy(d, me).start()
        return _

    lax.fori_loop(1, n, send_acts, 0)

    load_rows.wait()
    high, low = split(rows[...])
    lhs[pl.ds(local_tokens, local_rows), :] = high
    lhs[pl.ds(local_tokens + local_rows, local_rows), :] = low
    load_grads.wait()
    update[...] = jnp.zeros_like(update)

    def rotate(c):
        tile = 256

        def part(t, _):
            columns = pl.ds(pl.multiple_of(t * tile, 128), tile)
            out = jnp.dot(lhs[...], whole[c, :, columns], preferred_element_type=jnp.float32)
            turned = out[:local_tokens]
            eigen_sums[c, me, :, columns] = jnp.sum(turned * turned, axis=0, keepdims=True)
            coeffs[c, :, columns] = out[local_tokens : local_tokens + local_rows] + out[local_tokens + local_rows :]
            return _

        lax.fori_loop(0, width // tile, part, 0)

        def send(d, _):
            eigen_copy(c, d, me).start()
            return _

        lax.fori_loop(1, n, send, 0)

    def finish_acts():
        def arrive(d, _):
            act_copy(d, (me + n - d) % n).wait_recv()
            return _

        lax.fori_loop(1, n, arrive, 0)
        total = act_sums[0]
        for owner in range(1, n):
            total = total + act_sums[owner]
        wide = total.shape[1]
        block = 512
        picked = jnp.zeros((local_rows, 1), jnp.float32)
        for b in range(wide // block):
            at = lax.broadcasted_iota(jnp.int32, (local_rows, block), 1) + b * block
            row = lax.broadcasted_iota(jnp.int32, (local_rows, block), 0) + me * local_rows
            mine = jnp.where(at == row, jnp.broadcast_to(total[:, b * block : (b + 1) * block], at.shape), 0.0)
            picked = picked + jnp.sum(mine, axis=1, keepdims=True)
        square = (local_rows, local_rows)
        same = lax.broadcasted_iota(jnp.int32, square, 0) == lax.broadcasted_iota(jnp.int32, square, 1)
        old = jnp.sum(jnp.where(same, jnp.broadcast_to(a_old[...], square), 0.0), axis=1, keepdims=True)
        new = RETAIN * old + (1.0 - RETAIN) * (picked / tokens)
        column[...] = jnp.broadcast_to(new, column.shape)
        a_new[...] = jnp.sum(jnp.where(same, jnp.broadcast_to(new, square), 0.0), axis=0, keepdims=True)

    def back(c):
        def arrive(d, _):
            eigen_copy(c, d, (me + n - d) % n).wait_recv()
            return _

        lax.fori_loop(1, n, arrive, 0)
        total = eigen_sums[c, 0]
        for owner in range(1, n):
            total = total + eigen_sums[c, owner]
        columns = pl.ds(pl.multiple_of(c * width, 128), width)
        values = RETAIN * eigen_old[:, columns] + (1.0 - RETAIN) * (total / tokens)
        eigen_new[:, columns] = values
        scaled = coeffs[c] / (column[:, 0:1] * values + DAMPING)
        top, bottom = split(scaled)
        damped[pl.ds(0, local_rows), :] = top
        damped[pl.ds(local_rows, local_rows), :] = bottom
        tile = 256

        def part(t, _):
            here = pl.ds(pl.multiple_of(t * tile, 128), tile)
            out = lax.dot_general(
                damped[...], whole[c, here, :], (((1,), (1,)), ((), ())), preferred_element_type=jnp.float32
            )
            update[:, here] += out[:local_rows] + out[local_rows:]
            return _

        lax.fori_loop(0, features // tile, part, 0)

    def step(i, carry):
        @pl.when(i < CHUNKS)
        def _():
            for present, further, onward, over, beside in layer_moves(i):
                run(present, functools.partial(pass_on, over, beside))
                run(further, onward.start)

        @pl.when(i + AHEAD < CHUNKS)
        def _():
            send_own(i + AHEAD)

        @pl.when(jnp.logical_and(i >= 1, i <= CHUNKS))
        def _():
            c = i - 1
            for copy in across_moves(c):
                copy.wait_recv()
                copy.start()
            for at_side in range(2):
                for d in range(layers):
                    owner = index(d, at_side, 1 - core)
                    move(c, owner, sibling, 0).wait_recv()
            rotate(c)

        @pl.when(i == 1)
        def _():
            finish_acts()

        @pl.when(i >= 2)
        def _():
            back(i - 2)

        return carry

    lax.fori_loop(0, CHUNKS + 2, step, 0)

    def drain(c, _):
        for condition, copy in own_moves(c):
            run(condition, copy.wait_send)
        for present, further, onward, over, beside in layer_moves(c):
            run(present, over.wait_send)
            run(present, beside.wait_send)
            run(further, onward.wait_send)
        for copy in across_moves(c):
            copy.wait_send()

        def sent(d, _):
            eigen_copy(c, d, me).wait_send()
            return _

        return lax.fori_loop(1, n, sent, _)

    lax.fori_loop(0, CHUNKS, drain, 0)

    def act_sent(d, _):
        act_copy(d, me).wait_send()
        return _

    lax.fori_loop(1, n, act_sent, 0)


def fused(acts, out_grads, a_old, eigen_old, gradient, basis):
    n = lax.axis_size("dp")
    tokens = acts.shape[0] * n
    height, features = basis.shape
    width = features // CHUNKS
    local_rows = gradient.shape[0]
    depth = out_grads.shape[0] + 2 * local_rows
    wide = acts.shape[1]
    hbm = pl.BlockSpec(memory_space=pl.ANY)
    vmem = pl.BlockSpec(memory_space=pltpu.VMEM)
    copies = 7 * (n // 4)
    a_new, eigen_new, update = pl.pallas_call(
        functools.partial(kernel, n, tokens),
        out_shape=(
            jax.ShapeDtypeStruct((1, local_rows), jnp.float32),
            jax.ShapeDtypeStruct((1, features), jnp.float32),
            jax.ShapeDtypeStruct((local_rows, features), jnp.float32),
        ),
        in_specs=[hbm, hbm, hbm, vmem, vmem, vmem],
        out_specs=(vmem, vmem, vmem),
        scratch_shapes=[
            pltpu.VMEM((CHUNKS, features, width), jnp.bfloat16),
            pltpu.VMEM(acts.shape, jnp.bfloat16),
            pltpu.VMEM((depth, features), jnp.bfloat16),
            pltpu.VMEM(gradient.shape, jnp.float32),
            pltpu.VMEM((CHUNKS, local_rows, width), jnp.float32),
            pltpu.VMEM((2 * local_rows, width), jnp.bfloat16),
            pltpu.VMEM((local_rows, 128), jnp.float32),
            pltpu.VMEM((n, 1, wide), jnp.float32),
            pltpu.VMEM((CHUNKS, n, 1, width), jnp.float32),
            pltpu.SemaphoreType.DMA((3,)),
            pltpu.SemaphoreType.DMA((CHUNKS, copies)),
            pltpu.SemaphoreType.DMA((CHUNKS, n)),
            pltpu.SemaphoreType.DMA((n,)),
            pltpu.SemaphoreType.DMA((n,)),
            pltpu.SemaphoreType.DMA((CHUNKS, n)),
            pltpu.SemaphoreType.DMA((CHUNKS, n)),
        ],
        compiler_params=pltpu.CompilerParams(
            collective_id=0, has_side_effects=True, vmem_limit_bytes=56 * 1024 * 1024
        ),
    )(acts, out_grads, gradient, a_old.reshape(1, -1), eigen_old.reshape(1, -1), basis)
    return a_new.reshape(-1), eigen_new.reshape(-1), update


def plain(acts, out_grads, a_old, eigen_old, gradient, basis):
    tokens = acts.shape[0] * lax.axis_size("dp")
    own_rows = a_old.shape[0]
    act_float = acts.astype(jnp.float32)
    act_part = jnp.sum(act_float * act_float, axis=0)
    shard_rows = lax.all_gather(basis, "dp", axis=0, tiled=True)
    token_part = jnp.dot(out_grads, shard_rows, preferred_element_type=jnp.float32)
    row_part = jnp.dot(gradient, shard_rows.astype(jnp.float32), precision=lax.Precision.HIGHEST)
    eigen_part = jnp.sum(token_part * token_part, axis=0)
    act_whole, eigen_total = lax.psum((act_part, eigen_part), "dp")
    act_total = lax.dynamic_slice_in_dim(act_whole, lax.axis_index("dp") * own_rows, own_rows, 0)
    a_new = RETAIN * a_old + (1.0 - RETAIN) * (act_total / tokens)
    eigen_new = RETAIN * eigen_old + (1.0 - RETAIN) * (eigen_total / tokens)
    scaled = row_part / (a_new[:, None] * eigen_new[None, :] + DAMPING)
    update = jnp.einsum("ik,jk->ij", scaled, shard_rows.astype(jnp.float32), precision=lax.Precision.HIGHEST)
    return (a_new, eigen_new, update)


def solution(mesh):
    return jax.shard_map(
        fused if mesh.shape["dp"] == 16 else plain,
        mesh=mesh,
        in_specs=(
            P(("groups", "dp"), None),
            P(("groups", "dp"), None),
            P(("groups", "dp")),
            P("groups"),
            P(("groups", "dp"), None),
            P(("groups", "dp"), None),
        ),
        out_specs=(P(("groups", "dp")), P("groups"), P(("groups", "dp"), None)),
        check_vma=False,
    )
```

```python
import functools

import jax
import jax.numpy as jnp
from jax import lax
from jax.experimental import pallas as pl
from jax.experimental.pallas import tpu as pltpu
from jax.sharding import PartitionSpec as P

RETAIN = 0.9
DAMPING = 0.001
MESH = pl.DeviceIdType.MESH
CHUNKS = 5
AHEAD = 2
BACK = 2


def split(x):
    high = x.astype(jnp.bfloat16)
    low = (x - high.astype(jnp.float32)).astype(jnp.bfloat16)
    return high, low


def span(rows):
    return (rows + 64 + 127) // 128 * 128


def kernel(
    n, tokens, acts_hbm, grads_hbm, rows_hbm, a_old, eigen_old, basis,
    a_new, eigen_new, update,
    whole, acts, lhs, rows, coeffs, damped, column, act_row, act_sums, eigen_sums,
    load_sem, send_sem, recv_sem, act_send, act_recv, eigen_send, eigen_recv,
):
    me = lax.axis_index("dp")
    group = lax.axis_index("groups")
    core = me % 2
    side = (me // 2) % 2
    layer = me // 4
    layers = n // 4
    height, features = basis.shape
    width = features // CHUNKS
    local_tokens = grads_hbm.shape[0]
    local_rows = rows_hbm.shape[0]

    def index(at_layer, at_side, at_core):
        return (at_layer * 2 + at_side) * 2 + at_core

    sibling = index(layer, side, 1 - core)
    across = index(layer, 1 - side, core)

    load_acts = pltpu.make_async_copy(acts_hbm, acts, load_sem.at[0])
    load_grads = pltpu.make_async_copy(grads_hbm, lhs.at[pl.ds(0, local_tokens), :], load_sem.at[1])
    load_rows = pltpu.make_async_copy(rows_hbm, rows, load_sem.at[2])

    barrier = pltpu.get_barrier_semaphore()

    def greet(d, _):
        pl.semaphore_signal(barrier, inc=1, device_id=(group, (me + d) % n), device_id_type=MESH)
        return _

    load_acts.start()
    load_rows.start()
    load_grads.start()
    lax.fori_loop(1, n, greet, 0)
    pl.semaphore_wait(barrier, n - 1)

    def slot(c, owner):
        return whole.at[c, pl.ds(pl.multiple_of(owner * height, 16), height), :]

    def move(c, owner, target, which, own=False):
        source = basis.at[:, pl.ds(pl.multiple_of(c * width, 128), width)] if own else slot(c, owner)
        return pltpu.make_async_remote_copy(
            src_ref=source,
            dst_ref=slot(c, owner),
            send_sem=send_sem.at[c, which],
            recv_sem=recv_sem.at[c, owner],
            device_id=(group, target),
            device_id_type=MESH,
        )

    def own_moves(c):
        return [
            (layer < layers - 1, move(c, me, me + 4, 0, True)),
            (layer > 0, move(c, me, me - 4, 1, True)),
            (None, move(c, me, across, 2, True)),
            (None, move(c, me, sibling, 3, True)),
        ]

    def layer_moves(c):
        out = []
        for d in range(1, layers):
            for below in (True, False):
                base = 4 + 3 * (2 * (d - 1) + (0 if below else 1))
                owner = me - 4 * d if below else me + 4 * d
                onward = me + 4 if below else me - 4
                present = layer >= d if below else layer + d < layers
                further = layer < layers - 1 if below else layer > 0
                out.append((
                    present,
                    jnp.logical_and(present, further),
                    move(c, owner, onward, base),
                    move(c, owner, across, base + 1),
                    move(c, owner, sibling, base + 2),
                ))
        return out

    def across_moves(c):
        base = 4 + 6 * (layers - 1)
        return [
            move(c, index((layer + layers - d) % layers, 1 - side, core), sibling, base + d)
            for d in range(layers)
        ]

    def run(condition, action):
        if condition is None:
            action()
        else:
            pl.when(condition)(action)

    def send_own(c):
        for condition, copy in own_moves(c):
            run(condition, copy.start)
        whole[c, pl.ds(pl.multiple_of(me * height, 16), height), :] = basis[
            :, pl.ds(pl.multiple_of(c * width, 128), width)
        ]

    def pass_on(over, beside, further, onward):
        over.wait_recv()
        run(further, onward.start)
        over.start()
        beside.start()

    for c in range(AHEAD):
        send_own(c)

    load_acts.wait()
    act_width = 512

    def add_acts(b, _):
        columns = pl.ds(pl.multiple_of(b * act_width, 128), act_width)
        block = acts[:, columns].astype(jnp.float32)
        act_row[:, columns] = jnp.sum(block * block, axis=0, keepdims=True)
        return _

    lax.fori_loop(0, acts.shape[1] // act_width, add_acts, 0)

    def window(device):
        start = (device * local_rows) // 128 * 128
        return pl.ds(pl.multiple_of(start, 128), span(local_rows))

    def act_copy(d, owner):
        return pltpu.make_async_remote_copy(
            src_ref=act_row.at[:, window((me + d) % n)],
            dst_ref=act_sums.at[owner],
            send_sem=act_send.at[d],
            recv_sem=act_recv.at[owner],
            device_id=(group, (me + d) % n),
            device_id_type=MESH,
        )

    def eigen_copy(c, d, owner):
        return pltpu.make_async_remote_copy(
            src_ref=eigen_sums.at[c, owner],
            dst_ref=eigen_sums.at[c, owner],
            send_sem=eigen_send.at[c, d],
            recv_sem=eigen_recv.at[c, owner],
            device_id=(group, (me + d) % n),
            device_id_type=MESH,
        )

    def send_acts(d, _):
        act_copy(d, me).start()
        return _

    lax.fori_loop(1, n, send_acts, 0)
    act_sums[me] = act_row[:, window(me)]

    def prepare():
        load_rows.wait()
        high, low = split(rows[...])
        lhs[pl.ds(local_tokens, local_rows), :] = high
        lhs[pl.ds(local_tokens + local_rows, local_rows), :] = low
        load_grads.wait()
        update[...] = jnp.zeros_like(update)

    def rotate(c, first, last):
        tile = 256

        def part(t, _):
            columns = pl.ds(pl.multiple_of(t * tile, 128), tile)
            out = jnp.dot(lhs[...], whole[c, :, columns], preferred_element_type=jnp.float32)
            turned = out[:local_tokens]
            eigen_sums[c, me, :, columns] = jnp.sum(turned * turned, axis=0, keepdims=True)
            coeffs[c, :, columns] = out[local_tokens : local_tokens + local_rows] + out[local_tokens + local_rows :]
            return _

        lax.fori_loop(first, last, part, 0)

    def share(c):
        def send(d, _):
            eigen_copy(c, d, me).start()
            return _

        lax.fori_loop(1, n, send, 0)

    def finish_acts():
        def arrive(d, _):
            act_copy(d, (me + n - d) % n).wait_recv()
            return _

        lax.fori_loop(1, n, arrive, 0)
        total = act_sums[0]
        for owner in range(1, n):
            total = total + act_sums[owner]
        shape = (local_rows, total.shape[1])
        at = lax.broadcasted_iota(jnp.int32, shape, 1) + (me * local_rows) // 128 * 128
        row = lax.broadcasted_iota(jnp.int32, shape, 0) + me * local_rows
        picked = jnp.sum(jnp.where(at == row, jnp.broadcast_to(total, shape), 0.0), axis=1, keepdims=True)
        square = (local_rows, local_rows)
        same = lax.broadcasted_iota(jnp.int32, square, 0) == lax.broadcasted_iota(jnp.int32, square, 1)
        old = jnp.sum(jnp.where(same, jnp.broadcast_to(a_old[...], square), 0.0), axis=1, keepdims=True)
        new = RETAIN * old + (1.0 - RETAIN) * (picked / tokens)
        column[...] = jnp.broadcast_to(new, column.shape)
        a_new[...] = jnp.sum(jnp.where(same, jnp.broadcast_to(new, square), 0.0), axis=0, keepdims=True)

    def back(c):
        def arrive(d, _):
            eigen_copy(c, d, (me + n - d) % n).wait_recv()
            return _

        lax.fori_loop(1, n, arrive, 0)
        total = eigen_sums[c, 0]
        for owner in range(1, n):
            total = total + eigen_sums[c, owner]
        columns = pl.ds(pl.multiple_of(c * width, 128), width)
        values = RETAIN * eigen_old[:, columns] + (1.0 - RETAIN) * (total / tokens)
        eigen_new[:, columns] = values
        scaled = coeffs[c] / (column[:, 0:1] * values + DAMPING)
        top, bottom = split(scaled)
        damped[pl.ds(0, local_rows), :] = top
        damped[pl.ds(local_rows, local_rows), :] = bottom
        tile = 256

        def part(t, _):
            here = pl.ds(pl.multiple_of(t * tile, 128), tile)
            out = lax.dot_general(
                damped[...], whole[c, here, :], (((1,), (1,)), ((), ())), preferred_element_type=jnp.float32
            )
            update[:, here] += out[:local_rows] + out[local_rows:]
            return _

        lax.fori_loop(0, features // tile, part, 0)

    def forward(c, first, last):
        for present, further, onward, over, beside in layer_moves(c)[2 * first : 2 * last]:
            run(present, functools.partial(pass_on, over, beside, further, onward))

    def step(i, carry):
        inside = i < CHUNKS
        turning = jnp.logical_and(i >= 1, i <= CHUNKS)

        @pl.when(inside)
        def _():
            forward(i, 0, 1)

        @pl.when(i + AHEAD < CHUNKS)
        def _():
            send_own(i + AHEAD)

        @pl.when(i == 0)
        def _():
            prepare()

        @pl.when(turning)
        def _():
            for copy in across_moves(i - 1):
                copy.wait_recv()
                copy.start()

        @pl.when(inside)
        def _():
            forward(i, 1, 2)

        @pl.when(turning)
        def _():
            for at_side in range(2):
                for d in range(layers):
                    move(i - 1, index(d, at_side, 1 - core), sibling, 0).wait_recv()
            rotate(i - 1, 0, 1)

        @pl.when(inside)
        def _():
            forward(i, 2, 3)

        @pl.when(turning)
        def _():
            rotate(i - 1, 1, width // 256)
            share(i - 1)

        @pl.when(i == 1)
        def _():
            finish_acts()

        @pl.when(i >= BACK)
        def _():
            back(i - BACK)

        return carry

    lax.fori_loop(0, CHUNKS + BACK, step, 0)

    def drain(c, _):
        for condition, copy in own_moves(c):
            run(condition, copy.wait_send)
        for present, further, onward, over, beside in layer_moves(c):
            run(present, over.wait_send)
            run(present, beside.wait_send)
            run(further, onward.wait_send)
        for copy in across_moves(c):
            copy.wait_send()

        def sent(d, _):
            eigen_copy(c, d, me).wait_send()
            return _

        return lax.fori_loop(1, n, sent, _)

    lax.fori_loop(0, CHUNKS, drain, 0)

    def act_sent(d, _):
        act_copy(d, me).wait_send()
        return _

    lax.fori_loop(1, n, act_sent, 0)


def fused(acts, out_grads, a_old, eigen_old, gradient, basis):
    n = lax.axis_size("dp")
    tokens = acts.shape[0] * n
    height, features = basis.shape
    width = features // CHUNKS
    local_rows = gradient.shape[0]
    depth = out_grads.shape[0] + 2 * local_rows
    wide = acts.shape[1]
    hbm = pl.BlockSpec(memory_space=pl.ANY)
    vmem = pl.BlockSpec(memory_space=pltpu.VMEM)
    copies = 7 * (n // 4)
    a_new, eigen_new, update = pl.pallas_call(
        functools.partial(kernel, n, tokens),
        out_shape=(
            jax.ShapeDtypeStruct((1, local_rows), jnp.float32),
            jax.ShapeDtypeStruct((1, features), jnp.float32),
            jax.ShapeDtypeStruct((local_rows, features), jnp.float32),
        ),
        in_specs=[hbm, hbm, hbm, vmem, vmem, vmem],
        out_specs=(vmem, vmem, vmem),
        scratch_shapes=[
            pltpu.VMEM((CHUNKS, features, width), jnp.bfloat16),
            pltpu.VMEM(acts.shape, jnp.bfloat16),
            pltpu.VMEM((depth, features), jnp.bfloat16),
            pltpu.VMEM(gradient.shape, jnp.float32),
            pltpu.VMEM((CHUNKS, local_rows, width), jnp.float32),
            pltpu.VMEM((2 * local_rows, width), jnp.bfloat16),
            pltpu.VMEM((local_rows, 128), jnp.float32),
            pltpu.VMEM((1, wide), jnp.float32),
            pltpu.VMEM((n, 1, span(local_rows)), jnp.float32),
            pltpu.VMEM((CHUNKS, n, 1, width), jnp.float32),
            pltpu.SemaphoreType.DMA((3,)),
            pltpu.SemaphoreType.DMA((CHUNKS, copies)),
            pltpu.SemaphoreType.DMA((CHUNKS, n)),
            pltpu.SemaphoreType.DMA((n,)),
            pltpu.SemaphoreType.DMA((n,)),
            pltpu.SemaphoreType.DMA((CHUNKS, n)),
            pltpu.SemaphoreType.DMA((CHUNKS, n)),
        ],
        compiler_params=pltpu.CompilerParams(
            collective_id=0, has_side_effects=True, vmem_limit_bytes=56 * 1024 * 1024
        ),
    )(acts, out_grads, gradient, a_old.reshape(1, -1), eigen_old.reshape(1, -1), basis)
    return a_new.reshape(-1), eigen_new.reshape(-1), update


def plain(acts, out_grads, a_old, eigen_old, gradient, basis):
    tokens = acts.shape[0] * lax.axis_size("dp")
    own_rows = a_old.shape[0]
    act_float = acts.astype(jnp.float32)
    act_part = jnp.sum(act_float * act_float, axis=0)
    shard_rows = lax.all_gather(basis, "dp", axis=0, tiled=True)
    token_part = jnp.dot(out_grads, shard_rows, preferred_element_type=jnp.float32)
    row_part = jnp.dot(gradient, shard_rows.astype(jnp.float32), precision=lax.Precision.HIGHEST)
    eigen_part = jnp.sum(token_part * token_part, axis=0)
    act_whole, eigen_total = lax.psum((act_part, eigen_part), "dp")
    act_total = lax.dynamic_slice_in_dim(act_whole, lax.axis_index("dp") * own_rows, own_rows, 0)
    a_new = RETAIN * a_old + (1.0 - RETAIN) * (act_total / tokens)
    eigen_new = RETAIN * eigen_old + (1.0 - RETAIN) * (eigen_total / tokens)
    scaled = row_part / (a_new[:, None] * eigen_new[None, :] + DAMPING)
    update = jnp.einsum("ik,jk->ij", scaled, shard_rows.astype(jnp.float32), precision=lax.Precision.HIGHEST)
    return (a_new, eigen_new, update)


def solution(mesh):
    return jax.shard_map(
        fused if mesh.shape["dp"] == 16 else plain,
        mesh=mesh,
        in_specs=(
            P(("groups", "dp"), None),
            P(("groups", "dp"), None),
            P(("groups", "dp")),
            P("groups"),
            P(("groups", "dp"), None),
            P(("groups", "dp"), None),
        ),
        out_specs=(P(("groups", "dp")), P("groups"), P(("groups", "dp"), None)),
        check_vma=False,
    )
```
